32 devices in a mesh: dp: 8 (over z, y), seq: 4 (over x, core).
Axes of the slice: x: 2, y: 2, z: 4, core: 2. Of those that a mesh axis runs over, the one named last changes fastest.
Arguments:
- tokens: bfloat16 [4096, 1088], P(('dp', 'seq')), may hold values from -8 to 8
- segment_ids: int32 [8, 512], P('dp'), may hold values from 0 to 3, never falling along the last dimension, each value on 1 to 385 neighbouring positions
- attend_weight: bfloat16 [1088, 3, 1088], P('seq', None, 'dp'), may hold values from -2 to 2
- output_weight: bfloat16 [1088, 1088], P('seq', 'dp'), may hold values from -1 to 1
- expand_weight: bfloat16 [1088, 4352], P('seq', 'dp'), may hold values from -0.1875 to 0.1875
- shrink_weight: bfloat16 [4352, 1088], P('seq', 'dp'), may hold values from -0.09375 to 0.09375
- vectors: bfloat16 [13056], P(('dp', 'seq')), may hold values from -2 to 2
- cotangent: bfloat16 [4096, 1088], P(('dp', 'seq')), may hold values from -6 to 6
Outputs:
- mixed: bfloat16 [4096, 1088], P(('dp', 'seq'))
- tokens_grad: float32 [4096, 1088], P(('dp', 'seq'))
- attend_grad: float32 [1088, 3, 1088], P('seq', None, 'dp')
- output_grad: float32 [1088, 1088], P('seq', 'dp')
- expand_grad: float32 [1088, 4352], P('seq', 'dp')
- shrink_grad: float32 [4352, 1088], P('seq', 'dp')
- vectors_grad: float32 [13056], P(('dp', 'seq'))
The draws below stay inside these ranges and needn't reach their ends.
Inputs may be any that keep to these rules, and one draw needn't show every extreme that they name: `segment_ids`: in each group the numbers never fall, every number of 0 to 3 occurs, each sequence has 1 to 385 tokens and one has exactly 385.
All inputs are finite; a program needn't handle non-finite values.
Results may differ from the reference program's by a relative error of at most 0.0093.
Values may be sent and summed in bfloat16 or wider, within the bound.
A program may use at most 192 MiB of HBM per device.

```python
import math
import jax
import jax.numpy as jnp
import numpy as np
from jax import lax

D = 1088
H = 17
HD = 64
FF = 4352
SEGS = 4
GROUP_TOK = 512
MAXLEN = 385
TOKENS = 4096
N_DP = 8


def draw_tokens(key, part):
    base_key = jax.random.fold_in(key, 11)
    return jnp.clip(jax.random.normal(base_key, (TOKENS, D), jnp.float32), -6.0, 6.0).astype(jnp.bfloat16)


def draw_attend_weight(key, part):
    weights = jax.random.normal(jax.random.fold_in(key, 21), (D, 3, H, HD), jnp.float32) * D ** (-0.5)
    weights = jnp.clip(weights, -0.5, 0.5)
    return weights.reshape(D, 3, D).astype(jnp.bfloat16)


def draw_vectors(key, part):
    row_key = jax.random.fold_in(key, 31)
    gain_key = jax.random.fold_in(key, 32)
    tail_key = jax.random.fold_in(key, 33)
    table = jnp.clip(jax.random.normal(row_key, (8, D), jnp.float32) * 0.3, -1.5, 1.5)
    gains = jax.random.uniform(gain_key, (8, D), jnp.float32, 0.6, 1.4)
    tail = jnp.clip(jax.random.normal(tail_key, (FF,), jnp.float32) * 0.5, -2.0, 2.0)
    rows_index = jnp.arange(8)[:, None]
    is_gain = (rows_index == 0) | (rows_index == 5)
    table = jnp.where(is_gain, gains, table)
    return jnp.concatenate((table.reshape(-1), tail)).astype(jnp.bfloat16)


def strengthened(values, stream_key, source, target, parts, factor):
    owner, partner = [(jnp.arange(values.shape[dim]) // (values.shape[dim] // parts)).reshape([-1 if axis == dim else 1 for axis in range(values.ndim)]) for dim in (source, target)]
    chosen = jax.random.permutation(stream_key, parts)[partner]
    strong = (owner == chosen) | (owner == (partner + parts // 2) % parts)
    return jnp.where(strong, factor * values, values)


def levels(key, shape, pieces, low, top_value):
    loudness = 1.0
    for position, parts in pieces:
        draws = jax.random.uniform(jax.random.fold_in(jax.random.fold_in(key, 6), position), (parts,), jnp.float32, low / len(pieces), top_value / len(pieces))
        loudness = loudness * jnp.repeat(jnp.exp(draws), shape[position] // parts).reshape((-1,) + (1,) * (len(shape) - 1 - position))
    return loudness


def length_profile(amount, total, most, skew):
    loads = [(1 << 20) // math.isqrt(rank ** skew) + 1 for rank in range(2, amount + 1)]
    rest, holding = total - most - (amount - 1), [1] * (amount - 1)
    while rest > 0:
        free = [i for i in range(amount - 1) if holding[i] < most]
        mass, budget = sum([loads[i] for i in free]), rest
        for i in free:
            more = min(most - holding[i], max(1, budget * loads[i] // mass), rest)
            holding[i] = holding[i] + more
            rest = rest - more
    return np.array([most] + holding)


def ragged(key, count, total, reach, skew):
    if count == 2:
        one = jax.random.randint(key, (), max(1, total - reach), min(reach, total - 1) + 1)
        return jnp.stack([one, total - one])
    sizes = jnp.asarray(length_profile(count, total, reach, skew), jnp.int32)
    twos = (count - 1) // 2
    donor, receiver = sizes[1:1 + 2 * twos:2], sizes[2:2 + 2 * twos:2]
    margin = jnp.minimum(donor - 1, reach - receiver)
    moved = jax.random.randint(jax.random.fold_in(key, 1), (twos,), 0, 1 << 20) % (margin + 1)
    sizes = sizes.at[1:1 + 2 * twos:2].set(donor - moved).at[2:2 + 2 * twos:2].set(receiver + moved)
    return sizes[jax.random.permutation(jax.random.fold_in(key, 2), count)]


def gaussian(stream_key, shape, deviation, limit, cuts=(), held_as=jnp.bfloat16):
    array = jax.random.normal(stream_key, shape, jnp.float32) * deviation
    if len(cuts) > 0:
        array = levels(stream_key, shape, cuts, -0.22, 0.18) * array
    return jnp.clip(array, min=-limit, max=limit).astype(held_as)


def gaussian_with(rng, shape, scale, most, pieces, heavy, kind=jnp.bfloat16):
    entries = scale * jax.random.normal(rng, shape, jnp.float32)
    if pieces:
        entries = entries * levels(rng, shape, pieces, -0.22, 0.18)
    return jnp.clip(strengthened(entries, jax.random.fold_in(rng, 3), *heavy), -most, most).astype(kind)


def setup_inputs(seed: int = 0) -> dict:
    splits = jax.random.split(jax.random.key(seed), 9)
    tokens = draw_tokens(jax.random.fold_in(splits[8], 71), 0)
    segment_ids = jax.vmap(lambda own: jnp.searchsorted(jnp.cumsum(ragged(own, SEGS, GROUP_TOK, MAXLEN, 2)), jnp.arange(GROUP_TOK), side="right"))(jax.random.split(splits[1], N_DP)).reshape((N_DP, GROUP_TOK)).astype(jnp.int32)
    attend_weight = draw_attend_weight(jax.random.fold_in(splits[8], 71), 0)
    output_weight = gaussian(splits[3], (D, D), (D // 32) ** -0.5, 1.0, ((0, 4), (1, 8)))
    expand_weight = gaussian(splits[4], (D, FF), D ** -0.5, 0.1875, ((0, 4), (1, 8)))
    shrink_weight = gaussian(splits[5], (FF, D), FF ** -0.5, 0.09375, ((0, 4), (1, 8)))
    vectors = draw_vectors(jax.random.fold_in(splits[8], 71), 0)
    cotangent = gaussian_with(splits[7], (TOKENS, D), 1.0, 6.0, ((0, 32),), (0, 1, 32, 2.75))
    return {"tokens": tokens, "segment_ids": segment_ids, "attend_weight": attend_weight, "output_weight": output_weight, "expand_weight": expand_weight, "shrink_weight": shrink_weight, "vectors": vectors, "cotangent": cotangent}


EPS = 1e-05

def layer_norm(values):
    centre = values - lax.optimization_barrier(jnp.mean(values, axis=-1, keepdims=True))
    inverse = lax.rsqrt(lax.optimization_barrier(jnp.mean(centre * centre, axis=-1, keepdims=True)) + EPS)
    return (centre * inverse, inverse)

def norm_back(upstream, normed, inverse, gain):
    scaled = upstream * gain
    return (scaled - lax.optimization_barrier(jnp.mean(scaled, axis=-1, keepdims=True)) - normed * lax.optimization_barrier(jnp.mean(scaled * normed, axis=-1, keepdims=True))) * inverse

def gelu_parts(pre):
    normal_cdf = 0.5 * (1.0 + lax.erf(pre * 0.7071067811865476))
    density = jnp.exp(-0.5 * pre * pre) * 0.3989422804014327
    return (pre * normal_cdf, normal_cdf + pre * density)

def reference(tokens, segment_ids, attend_weight, output_weight, expand_weight, shrink_weight, vectors, cotangent):
    attend = attend_weight.reshape(D, 3 * D)
    output = output_weight
    expand = expand_weight
    shrink = shrink_weight
    table = vectors[:8 * D].astype(jnp.float32).reshape(8, D)
    fc_bias = vectors[8 * D:].astype(jnp.float32)
    places = jnp.arange(GROUP_TOK, dtype=jnp.int32)

    def group_step(carry, inputs):
        block, segment, upstream_low = inputs
        inputs32 = block.astype(jnp.float32)
        normed_one, inverse_one = layer_norm(inputs32)
        hidden_one = (normed_one * table[0] + table[1]).astype(jnp.bfloat16)
        projected = jnp.dot(hidden_one, attend, preferred_element_type=jnp.float32)
        queries = (projected[:, :D] + table[2]).astype(jnp.bfloat16)
        keys = projected[:, D:2 * D].astype(jnp.bfloat16)
        values = (projected[:, 2 * D:] + table[3]).astype(jnp.bfloat16)
        query_heads = queries.astype(jnp.float32).reshape(GROUP_TOK, H, HD)
        key_heads = keys.astype(jnp.float32).reshape(GROUP_TOK, H, HD)
        value_heads = values.astype(jnp.float32).reshape(GROUP_TOK, H, HD)
        allowed = (places[None, :] <= places[:, None]) & (segment[None, :] == segment[:, None])
        scores = jnp.einsum('thd,ghd->htg', query_heads, key_heads) * 0.125
        scores = jnp.where(allowed[None], scores, -jnp.inf)
        peak = lax.optimization_barrier(jnp.max(scores, axis=-1, keepdims=True))
        log_total = peak + jnp.log(lax.optimization_barrier(jnp.sum(jnp.exp(scores - peak), axis=-1, keepdims=True)))
        probs = jnp.exp(scores - log_total)
        probs_low = probs.astype(jnp.bfloat16)
        context = jnp.einsum('htg,ghd->thd', probs_low.astype(jnp.float32), value_heads)
        context = context.reshape(GROUP_TOK, D).astype(jnp.bfloat16)
        residual = inputs32 + jnp.dot(context, output, preferred_element_type=jnp.float32) + table[4]
        normed_two, inverse_two = layer_norm(residual)
        hidden_two = (normed_two * table[5] + table[6]).astype(jnp.bfloat16)
        pre = jnp.dot(hidden_two, expand, preferred_element_type=jnp.float32) + fc_bias
        activated, slope = gelu_parts(pre)
        activated_low = activated.astype(jnp.bfloat16)
        mixed = (residual + jnp.dot(activated_low, shrink, preferred_element_type=jnp.float32) + table[7]).astype(jnp.bfloat16)
        upstream = upstream_low.astype(jnp.float32)
        shrink_grad = jnp.dot(activated_low.T, upstream_low, preferred_element_type=jnp.float32)
        pre_grad = jnp.dot(upstream_low, shrink.T, preferred_element_type=jnp.float32) * slope
        pre_low = pre_grad.astype(jnp.bfloat16)
        expand_grad = jnp.dot(hidden_two.T, pre_low, preferred_element_type=jnp.float32)
        hidden_two_grad = jnp.dot(pre_low, expand.T, preferred_element_type=jnp.float32)
        residual_grad = upstream + norm_back(hidden_two_grad, normed_two, inverse_two, table[5])
        residual_low = residual_grad.astype(jnp.bfloat16)
        output_grad = jnp.dot(context.T, residual_low, preferred_element_type=jnp.float32)
        context_grad = jnp.dot(residual_low, output.T, preferred_element_type=jnp.float32).astype(jnp.bfloat16)
        grad_heads = context_grad.astype(jnp.float32).reshape(GROUP_TOK, H, HD)
        context_heads = context.astype(jnp.float32).reshape(GROUP_TOK, H, HD)
        prob_grad = jnp.einsum('thd,ghd->htg', grad_heads, value_heads)
        row_dots = jnp.einsum('thd,thd->ht', grad_heads, context_heads)[:, :, None]
        score_grad = (probs * (prob_grad - row_dots)).astype(jnp.bfloat16).astype(jnp.float32)
        query_grad = (jnp.einsum('htg,ghd->thd', score_grad, key_heads) * 0.125).reshape(GROUP_TOK, D)
        key_grad = (jnp.einsum('htg,thd->ghd', score_grad, query_heads) * 0.125).reshape(GROUP_TOK, D)
        value_grad = jnp.einsum('htg,thd->ghd', probs_low.astype(jnp.float32), grad_heads).reshape(GROUP_TOK, D)
        joined_low = jnp.concatenate((query_grad, key_grad, value_grad), axis=1).astype(jnp.bfloat16)
        attend_grad = jnp.dot(hidden_one.T, joined_low, preferred_element_type=jnp.float32)
        hidden_one_grad = jnp.dot(joined_low, attend.T, preferred_element_type=jnp.float32)
        tokens_grad = residual_grad + norm_back(hidden_one_grad, normed_one, inverse_one, table[0])
        vector_rows = jnp.stack((lax.optimization_barrier(jnp.sum(hidden_one_grad * normed_one, axis=0)), lax.optimization_barrier(jnp.sum(hidden_one_grad, axis=0)), lax.optimization_barrier(jnp.sum(query_grad, axis=0)), lax.optimization_barrier(jnp.sum(value_grad, axis=0)), lax.optimization_barrier(jnp.sum(residual_grad, axis=0)), lax.optimization_barrier(jnp.sum(hidden_two_grad * normed_two, axis=0)), lax.optimization_barrier(jnp.sum(hidden_two_grad, axis=0)), lax.optimization_barrier(jnp.sum(upstream, axis=0))))
        fc_grad = lax.optimization_barrier(jnp.sum(pre_grad, axis=0))
        updated = (carry[0] + attend_grad, carry[1] + output_grad, carry[2] + expand_grad, carry[3] + shrink_grad, carry[4] + vector_rows, carry[5] + fc_grad)
        return (updated, (mixed, tokens_grad))
    start = (jnp.zeros((D, 3 * D), jnp.float32), jnp.zeros((D, D), jnp.float32), jnp.zeros((D, FF), jnp.float32), jnp.zeros((FF, D), jnp.float32), jnp.zeros((8, D), jnp.float32), jnp.zeros((FF,), jnp.float32))
    totals, (mixed, tokens_grad) = lax.scan(group_step, start, (tokens.reshape(N_DP, GROUP_TOK, D), segment_ids, cotangent.reshape(N_DP, GROUP_TOK, D)))
    vectors_grad = jnp.concatenate((totals[4].reshape(-1), totals[5]))
    return (mixed.reshape(TOKENS, D), tokens_grad.reshape(TOKENS, D), totals[0].reshape(D, 3, D), totals[1], totals[2], totals[3], vectors_grad)
```

```python
import math
import jax
import jax.numpy as jnp
from jax import lax
from jax.sharding import PartitionSpec as P

D = 1088
H = 17
HD = 64
FF = 4352
EPS = 1e-05
BF = jnp.bfloat16
F32 = jnp.float32


def layer_norm(values):
    centre = values - jnp.mean(values, axis=-1, keepdims=True)
    inverse = lax.rsqrt(jnp.mean(centre * centre, axis=-1, keepdims=True) + EPS)
    return (centre * inverse, inverse)


def norm_back(upstream, normed, inverse, gain):
    scaled = upstream * gain
    return (
        scaled
        - jnp.mean(scaled, axis=-1, keepdims=True)
        - normed * jnp.mean(scaled * normed, axis=-1, keepdims=True)
    ) * inverse


def gelu_parts(pre):
    normal_cdf = 0.5 * (1.0 + lax.erf(pre * 0.7071067811865476))
    density = jnp.exp(-0.5 * pre * pre) * 0.3989422804014327
    return (pre * normal_cdf, normal_cdf + pre * density)


def gather_seq(values):
    return lax.all_gather(values, "seq", axis=0, tiled=False)


def gather_dp(values):
    return lax.all_gather(values, "dp", axis=0, tiled=False)


def swap_seq(values):
    return lax.all_to_all(values, "seq", split_axis=0, concat_axis=0, tiled=True)


def sum_seq(values):
    return lax.psum_scatter(values, "seq", scatter_dimension=0, tiled=False).astype(F32)


def sum_dp(values):
    return lax.psum_scatter(values, "dp", scatter_dimension=0, tiled=False).astype(F32)


def dot(a, b, ca, cb):
    return lax.dot_general(a, b, (((ca,), (cb,)), ((), ())), preferred_element_type=F32)


def up(value, step):
    return -(-value // step) * step


def padded(values, shape):
    return jnp.pad(values, [(0, n - m) for m, n in zip(values.shape, shape)])


def body(
    tokens,
    segment_ids,
    attend_weight,
    output_weight,
    expand_weight,
    shrink_weight,
    vectors,
    cotangent,
):
    rows = tokens.shape[0]
    S = lax.axis_size("seq")
    N = lax.axis_size("dp")
    group = rows * S
    place = lax.axis_index("seq")
    dr = D // S
    dc = D // N
    fc = FF // N
    hq = FF // S
    heads = -(-H // S)
    hw = heads * HD
    vn = vectors.shape[0]
    row_pad = up(dr, 16)
    cols = 12 * dc
    col_pad = up(cols, 128)

    shrink_split = shrink_weight.reshape(4, dr, dc).transpose(1, 0, 2).reshape(dr, 4 * dc)
    packed = jnp.concatenate(
        (expand_weight, attend_weight.reshape(dr, 3 * dc), output_weight, shrink_split), axis=1
    )
    packed = padded(packed, (row_pad, col_pad))
    packed = jnp.concatenate((packed, padded(vectors[None], (16, col_pad))), axis=0)
    whole = gather_dp(packed)
    both = gather_seq(jnp.concatenate((tokens, cotangent), axis=1))
    tokens_all = both[:, :, :D].reshape(group, D)
    upstream_all = both[:, :, D:].reshape(group, D)

    mine = whole[:, :dr]
    expand_rows = mine[:, :, : 4 * dc].transpose(1, 0, 2).reshape(dr, FF)
    attend_rows = (
        mine[:, :, 4 * dc : 7 * dc].reshape(N, dr, 3, dc).transpose(1, 2, 0, 3).reshape(dr, 3, D)
    )
    output_rows = mine[:, :, 7 * dc : 8 * dc].transpose(1, 0, 2).reshape(dr, D)
    shrink_rows = (
        mine[:, :, 8 * dc : 12 * dc].reshape(N, dr, 4, dc).transpose(2, 1, 0, 3).reshape(4 * dr, D)
    )

    attend_out = (
        padded(attend_rows, (dr, 3, S * hw)).reshape(dr, 3, S, hw).transpose(2, 0, 1, 3)
    ).reshape(S, dr, 3 * hw)
    attend_cols = swap_seq(attend_out).reshape(D, 3 * hw)
    expand_out = expand_rows.reshape(dr, S, hq).transpose(1, 0, 2)
    expand_cols = swap_seq(expand_out).reshape(D, hq)
    output_and = jnp.concatenate(
        (padded(output_rows, (row_pad, D)), padded(whole[:, row_pad, :vn], (up(N, 16), D))), axis=0
    )
    output_and_all = gather_seq(output_and)
    output_all = output_and_all[:, :dr].reshape(D, D)
    output_heads = lax.dynamic_slice_in_dim(
        padded(output_all, (S * hw, D)), place * hw, hw, 0
    )
    flat = output_and_all[:, row_pad : row_pad + N, :vn].transpose(1, 0, 2).reshape(-1)
    table = flat[: 8 * D].astype(F32).reshape(8, D)
    fc_bias = flat[8 * D :].astype(F32)

    def head_part(vector):
        return lax.dynamic_slice_in_dim(padded(vector, (S * hw,)), place * hw, hw, 0)

    normed_all, _ = layer_norm(tokens_all.astype(F32))
    hidden_one_all = (normed_all * table[0] + table[1]).astype(BF)
    inputs32 = tokens.astype(F32)
    normed_one, inverse_one = layer_norm(inputs32)
    projected = dot(hidden_one_all, attend_cols, 1, 0)
    bias = jnp.concatenate((head_part(table[2]), jnp.zeros((hw,), F32), head_part(table[3])))
    triple = (projected + bias).astype(BF).reshape(group, 3, heads, HD).transpose(1, 2, 0, 3)
    query, key, value = triple[0], triple[1], triple[2]
    segment = segment_ids.reshape(-1)
    pos = jnp.arange(group, dtype=jnp.int32)
    allowed = (pos[None, :] <= pos[:, None]) & (segment[None, :] == segment[:, None])
    scores = jnp.einsum("htd,hgd->htg", query, key, preferred_element_type=F32) * 0.125
    scores = jnp.where(allowed[None], scores, -jnp.inf)
    peak = jnp.max(scores, axis=-1, keepdims=True)
    unscaled = jnp.exp(scores - peak)
    probs = unscaled / jnp.sum(unscaled, axis=-1, keepdims=True)
    probs_low = probs.astype(BF)
    context = jnp.einsum("htg,hgd->htd", probs_low, value, preferred_element_type=F32).astype(BF)
    context_cols = context.transpose(1, 0, 2).reshape(group, hw)
    attn = dot(context_cols, output_heads, 1, 0).astype(BF)
    residual = inputs32 + sum_seq(attn.reshape(S, rows, D)) + table[4]
    normed_two, inverse_two = layer_norm(residual)
    hidden_two = (normed_two * table[5] + table[6]).astype(BF)
    hidden_two_all = gather_seq(hidden_two).reshape(group, D)
    hidden_bias = lax.dynamic_slice_in_dim(fc_bias, place * hq, hq, 0)
    pre = dot(hidden_two_all, expand_cols, 1, 0) + hidden_bias
    activated, slope = gelu_parts(pre)
    activated_low = activated.astype(BF)
    branch = dot(activated_low, shrink_rows, 1, 0).astype(BF)
    upstream = cotangent.astype(F32)
    pre_grad = dot(upstream_all, shrink_rows, 1, 1) * slope
    pre_low = pre_grad.astype(BF)
    hidden_two_grad = sum_seq(dot(pre_low, expand_cols, 1, 1).astype(BF).reshape(S, rows, D))
    mixed = (residual + sum_seq(branch.reshape(S, rows, D)) + table[7]).astype(BF)
    shrink_grad = dot(activated_low, upstream_all, 0, 0).astype(BF)
    expand_grad = dot(hidden_two_all, pre_low, 0, 0).astype(BF)
    expand_grad = swap_seq(expand_grad.reshape(S, dr, hq))
    residual_grad = upstream + norm_back(hidden_two_grad, normed_two, inverse_two, table[5])
    residual_all = gather_seq(residual_grad.astype(BF)).reshape(group, D)
    grad = dot(residual_all, output_heads, 1, 1).astype(BF)
    grad = grad.reshape(group, heads, HD).transpose(1, 0, 2)
    row_dots = jnp.sum(grad.astype(F32) * context.astype(F32), axis=-1, keepdims=True)
    prob_grad = jnp.einsum("htd,hgd->htg", grad, value, preferred_element_type=F32)
    score_grad = (probs * (prob_grad - row_dots)).astype(BF)
    query_grad = jnp.einsum("htg,hgd->thd", score_grad, key, preferred_element_type=F32) * 0.125
    key_grad = jnp.einsum("htg,htd->ghd", score_grad, query, preferred_element_type=F32) * 0.125
    value_grad = jnp.einsum("htg,htd->ghd", probs_low, grad, preferred_element_type=F32)
    query_grad, key_grad, value_grad = (
        g.reshape(group, hw) for g in (query_grad, key_grad, value_grad)
    )
    joined = jnp.concatenate((query_grad, key_grad, value_grad), axis=1).astype(BF)
    hidden_one_grad = sum_seq(dot(joined, attend_cols, 1, 1).astype(BF).reshape(S, rows, D))
    attend_grad = dot(hidden_one_all, joined, 0, 0).astype(BF)
    attend_grad = swap_seq(attend_grad.reshape(S, dr, 3 * hw))
    output_grad = dot(context_cols, residual_all, 0, 0).astype(BF)
    output_grad = lax.dynamic_slice_in_dim(
        gather_seq(output_grad).reshape(S * hw, D), place * dr, dr, 0
    )
    tokens_grad = residual_grad + norm_back(hidden_one_grad, normed_one, inverse_one, table[0])

    attend_grad = attend_grad.reshape(S, dr, 3, hw).transpose(1, 2, 0, 3).reshape(dr, 3, S * hw)
    attend_grad = attend_grad[:, :, :D].reshape(dr, 3, N, dc).transpose(2, 0, 1, 3)
    expand_grad = expand_grad.reshape(S, dr, N // S, fc).transpose(0, 2, 1, 3).reshape(N, dr, fc)
    output_grad = output_grad.reshape(dr, N, dc).transpose(1, 0, 2)
    shrink_grad = shrink_grad.reshape(4, dr, N, dc).transpose(2, 1, 0, 3).reshape(N, dr, 4 * dc)
    packed_grad = jnp.concatenate(
        (expand_grad, attend_grad.reshape(N, dr, 3 * dc), output_grad, shrink_grad), axis=2
    )

    def spread(vector, total, start):
        return lax.dynamic_update_slice(jnp.zeros((total,), F32), vector, (start,))

    vector_grad = jnp.concatenate(
        (
            jnp.sum(hidden_one_grad * normed_one, axis=0),
            jnp.sum(hidden_one_grad, axis=0),
            spread(jnp.sum(query_grad, axis=0), S * hw, place * hw)[:D],
            spread(jnp.sum(value_grad, axis=0), S * hw, place * hw)[:D],
            jnp.sum(residual_grad, axis=0),
            jnp.sum(hidden_two_grad * normed_two, axis=0),
            jnp.sum(hidden_two_grad, axis=0),
            jnp.sum(upstream, axis=0),
            spread(jnp.sum(pre_grad, axis=0), FF, place * hq),
        )
    )
    by_owner = vector_grad.reshape(N, S, vn).transpose(1, 0, 2)
    by_owner = padded(by_owner, (S, up(N, 16), up(vn, 128)))
    vector_part = sum_seq(by_owner)[:N].astype(BF)
    vector_part = padded(vector_part[:, None, :], (N, 16, col_pad))
    packed_grad = jnp.concatenate(
        (padded(packed_grad, (N, row_pad, col_pad)), vector_part), axis=1
    )
    total = sum_dp(packed_grad)
    weight_sum = total[:dr]
    return (
        mixed,
        tokens_grad,
        weight_sum[:, 4 * dc : 7 * dc].reshape(dr, 3, dc),
        weight_sum[:, 7 * dc : 8 * dc],
        weight_sum[:, : 4 * dc],
        weight_sum[:, 8 * dc : 12 * dc].reshape(dr, 4, dc).transpose(1, 0, 2).reshape(4 * dr, dc),
        total[row_pad, :vn],
    )


def solution(mesh):
    return jax.shard_map(
        body,
        mesh=mesh,
        in_specs=(
            P(("dp", "seq"), None),
            P("dp", None),
            P("seq", None, "dp"),
            P("seq", "dp"),
            P("seq", "dp"),
            P("seq", "dp"),
            P(("dp", "seq")),
            P(("dp", "seq"), None),
        ),
        out_specs=(
            P(("dp", "seq"), None),
            P(("dp", "seq"), None),
            P("seq", None, "dp"),
            P("seq", "dp"),
            P("seq", "dp"),
            P("seq", "dp"),
            P(("dp", "seq")),
        ),
        check_vma=False,
    )
```

```python
import itertools
import math
import jax
import jax.numpy as jnp
from jax import lax
from jax.experimental import pallas as pl
from jax.experimental.pallas import tpu as pltpu
from jax.sharding import PartitionSpec as P

D = 1088
H = 17
HD = 64
FF = 4352
EPS = 1e-05
BF = jnp.bfloat16
F32 = jnp.float32


def layer_norm(values):
    centre = values - jnp.mean(values, axis=-1, keepdims=True)
    inverse = lax.rsqrt(jnp.mean(centre * centre, axis=-1, keepdims=True) + EPS)
    return (centre * inverse, inverse)


def norm_back(upstream, normed, inverse, gain):
    scaled = upstream * gain
    return (
        scaled
        - jnp.mean(scaled, axis=-1, keepdims=True)
        - normed * jnp.mean(scaled * normed, axis=-1, keepdims=True)
    ) * inverse


def gelu_parts(pre):
    normal_cdf = 0.5 * (1.0 + lax.erf(pre * 0.7071067811865476))
    density = jnp.exp(-0.5 * pre * pre) * 0.3989422804014327
    return (pre * normal_cdf, normal_cdf + pre * density)


MESH = pl.DeviceIdType.MESH
IDS = itertools.count()
LIMIT = 48 * 2**20


def greet(targets):
    barrier = pltpu.get_barrier_semaphore()
    for target in targets:
        pl.semaphore_signal(barrier, inc=1, device_id=target, device_id_type=MESH)
    pl.semaphore_wait(barrier, len(targets))


def send(src, dst, send_sem, recv_sem, target):
    copy = pltpu.make_async_remote_copy(
        src_ref=src,
        dst_ref=dst,
        send_sem=send_sem,
        recv_sem=recv_sem,
        device_id=target,
        device_id_type=MESH,
    )
    copy.start()
    return copy


def run_kernel(kernel, out_shapes, scratch, *args):
    return pl.pallas_call(
        kernel,
        out_shape=out_shapes,
        in_specs=[pl.BlockSpec(memory_space=pltpu.VMEM)] * len(args),
        out_specs=jax.tree.map(lambda _: pl.BlockSpec(memory_space=pltpu.VMEM), out_shapes),
        scratch_shapes=scratch,
        compiler_params=pltpu.CompilerParams(
            collective_id=next(IDS), has_side_effects=True, vmem_limit_bytes=LIMIT
        ),
    )(*args)


def dma(*shape):
    return pltpu.SemaphoreType.DMA(shape)


def gather_seq_steps(n, src, dst, local, sends, recvs):
    chips = n // 2
    me = lax.axis_index("seq")
    x, core = me // 2, me % 2
    other = {"seq": x * 2 + (1 - core)}
    own = pltpu.make_async_copy(src, dst.at[me], local)
    own.start()
    across = []
    for k in range(1, chips):
        target = {"seq": lax.rem(x + k, chips) * 2 + core}
        across.append(send(src, dst.at[me], sends.at[0, k], recvs.at[0, k], target))
    inner = [send(src, dst.at[me], sends.at[1, 0], recvs.at[1, 0], other)]

    def finish():
        for k in range(1, chips):
            across[k - 1].wait_recv()
            slot = lax.rem(x + chips - k, chips) * 2 + core
            inner.append(
                send(dst.at[slot], dst.at[slot], sends.at[1, k], recvs.at[1, k], other)
            )
        for copy in inner:
            copy.wait_recv()
        for copy in across + inner:
            copy.wait_send()
        own.wait()

    return finish


def seq_partners(n):
    me = lax.axis_index("seq")
    x, core = me // 2, me % 2
    chips = n // 2
    return [{"seq": x * 2 + (1 - core)}] + [
        {"seq": lax.rem(x + k, chips) * 2 + core} for k in range(1, chips)
    ]


def gather_seq(values):
    n = lax.axis_size("seq")

    def kernel(src, dst, local, sends, recvs):
        greet(seq_partners(n))
        gather_seq_steps(n, src, dst, local, sends, recvs)()

    return run_kernel(
        kernel,
        jax.ShapeDtypeStruct((n,) + values.shape, values.dtype),
        [pltpu.SemaphoreType.DMA, dma(2, n // 2), dma(2, n // 2)],
        values,
    )


def swap_seq(values):
    n = lax.axis_size("seq")

    def kernel(src, dst, local, sends, recvs):
        me = lax.axis_index("seq")
        greet([{"seq": lax.rem(me + k, n)} for k in range(1, n)])
        own = pltpu.make_async_copy(src.at[me], dst.at[me], local)
        own.start()
        copies = []
        for k in range(n - 1, 0, -1):
            to = lax.rem(me + k, n)
            copies.append(
                send(src.at[to], dst.at[me], sends.at[k - 1], recvs.at[k - 1], {"seq": to})
            )
        for copy in copies:
            copy.wait_recv()
        for copy in copies:
            copy.wait_send()
        own.wait()

    return run_kernel(
        kernel,
        jax.ShapeDtypeStruct(values.shape, values.dtype),
        [pltpu.SemaphoreType.DMA, dma(n - 1), dma(n - 1)],
        values,
    )


def sum_seq(values):
    return jnp.sum(swap_seq(values).astype(F32), axis=0)


def dp_layout():
    n = lax.axis_size("dp")
    wide = math.isqrt(n // 2)
    return n // wide, wide


def pieces(size, parts):
    units = size // 16
    edges = [units * i // parts * 16 for i in range(parts + 1)]
    return [(a, b - a) for a, b in zip(edges, edges[1:])]


def dp_partners(deep, wide):
    me = lax.axis_index("dp")
    z, y = me // wide, me % wide
    return [{"dp": lax.rem(z + k, deep) * wide + y} for k in range(1, deep)] + [
        {"dp": z * wide + lax.rem(y + k, wide)} for k in range(1, wide)
    ]


def gather_start(values, both):
    n = lax.axis_size("seq")
    deep, wide = dp_layout()
    chunks = pieces(values.shape[0], 3)

    def kernel(src, act, dst, act_dst, local, s_sends, s_recvs, z_send, z_recv, y_send, y_recv):
        me = lax.axis_index("dp")
        z, y = me // wide, me % wide
        greet(dp_partners(deep, wide) + seq_partners(n))
        finish = gather_seq_steps(n, act, act_dst, local.at[0], s_sends, s_recvs)
        own = pltpu.make_async_copy(src, dst.at[me], local.at[1])
        own.start()
        first, second = {}, []
        for c, (start, size) in enumerate(chunks):
            part = pl.ds(start, size)
            for k in range(1, deep):
                to = {"dp": lax.rem(z + k, deep) * wide + y}
                first[c, k] = send(
                    src.at[part], dst.at[me, part], z_send.at[c, k], z_recv.at[c, k], to
                )
            for j in range(1, wide):
                to = {"dp": z * wide + lax.rem(y + j, wide)}
                second.append(
                    send(
                        src.at[part], dst.at[me, part], y_send.at[c, j, 0], y_recv.at[c, j, 0], to
                    )
                )
        for c, (start, size) in enumerate(chunks):
            part = pl.ds(start, size)
            for k in range(1, deep):
                first[c, k].wait_recv()
                slot = lax.rem(z + deep - k, deep) * wide + y
                for j in range(1, wide):
                    to = {"dp": z * wide + lax.rem(y + j, wide)}
                    block = dst.at[slot, part]
                    second.append(
                        send(block, block, y_send.at[c, j, k], y_recv.at[c, j, k], to)
                    )
        finish()
        for copy in second:
            copy.wait_recv()
        for copy in list(first.values()) + second:
            copy.wait_send()
        own.wait()

    m = len(chunks)
    return run_kernel(
        kernel,
        (
            jax.ShapeDtypeStruct((deep * wide,) + values.shape, values.dtype),
            jax.ShapeDtypeStruct((n,) + both.shape, both.dtype),
        ),
        [dma(2), dma(2, n // 2), dma(2, n // 2)]
        + [dma(m, deep), dma(m, deep), dma(m, wide, deep), dma(m, wide, deep)],
        values,
        both,
    )


def sum_dp(values):
    deep, wide = dp_layout()
    rows, cols = values.shape[1:]
    chunks = pieces(rows, 3)

    def kernel(src, out, y_buf, z_out, z_buf, y_send, y_recv, z_send, z_recv):
        me = lax.axis_index("dp")
        z, y = me // wide, me % wide
        greet(dp_partners(deep, wide))
        order = list(range(1, deep)) + [0]
        first, second = {}, []
        for c, (start, size) in enumerate(chunks):
            part = pl.ds(start, size)
            for k in order:
                for j in range(1, wide):
                    there = lax.rem(y + j, wide)
                    first[c, k, j] = send(
                        src.at[lax.rem(z + k, deep) * wide + there, part],
                        y_buf.at[j - 1, k, part],
                        y_send.at[c, j, k],
                        y_recv.at[c, j, k],
                        {"dp": z * wide + there},
                    )
        for c, (start, size) in enumerate(chunks):
            part = pl.ds(start, size)
            for k in order:
                for j in range(1, wide):
                    first[c, k, j].wait_recv()
                block = lax.rem(z + k, deep) * wide + y

                @pl.loop(0, size // 16)
                def _(i):
                    strip = pl.ds(pl.multiple_of(start + i * 16, 16), 16)
                    total = src[block, strip, :].astype(F32)
                    for j in range(1, wide):
                        total = total + y_buf[j - 1, k, strip, :].astype(F32)
                    if k == 0:
                        out[strip, :] = total
                    else:
                        z_out[k - 1, strip, :] = total.astype(z_out.dtype)

                if k > 0:
                    second.append(
                        send(
                            z_out.at[k - 1, part],
                            z_buf.at[k - 1, part],
                            z_send.at[c, k],
                            z_recv.at[c, k],
                            {"dp": block},
                        )
                    )
        for c, (start, size) in enumerate(chunks):
            for k in range(1, deep):
                second[c * (deep - 1) + k - 1].wait_recv()

            @pl.loop(0, size // 16)
            def _(i):
                strip = pl.ds(pl.multiple_of(start + i * 16, 16), 16)
                total = out[strip, :]
                for k in range(1, deep):
                    total = total + z_buf[k - 1, strip, :].astype(F32)
                out[strip, :] = total

        for copy in list(first.values()) + second:
            copy.wait_send()

    m = len(chunks)
    return run_kernel(
        kernel,
        jax.ShapeDtypeStruct((rows, cols), F32),
        [
            pltpu.VMEM((wide - 1, deep, rows, cols), BF),
            pltpu.VMEM((deep - 1, rows, cols), BF),
            pltpu.VMEM((deep - 1, rows, cols), BF),
            dma(m, wide, deep),
            dma(m, wide, deep),
            dma(m, deep),
            dma(m, deep),
        ],
        values,
    )


def dot(a, b, ca, cb):
    return lax.dot_general(a, b, (((ca,), (cb,)), ((), ())), preferred_element_type=F32)


def up(value, step):
    return -(-value // step) * step


def padded(values, shape):
    return jnp.pad(values, [(0, n - m) for m, n in zip(values.shape, shape)])


def body(
    tokens,
    segment_ids,
    attend_weight,
    output_weight,
    expand_weight,
    shrink_weight,
    vectors,
    cotangent,
):
    rows = tokens.shape[0]
    S = lax.axis_size("seq")
    N = lax.axis_size("dp")
    group = rows * S
    place = lax.axis_index("seq")
    dr = D // S
    dc = D // N
    fc = FF // N
    hq = FF // S
    heads = -(-H // S)
    hw = heads * HD
    vn = vectors.shape[0]
    row_pad = up(dr, 16)
    cols = 12 * dc
    col_pad = up(cols, 128)

    shrink_split = shrink_weight.reshape(4, dr, dc).transpose(1, 0, 2).reshape(dr, 4 * dc)
    packed = jnp.concatenate(
        (expand_weight, attend_weight.reshape(dr, 3 * dc), output_weight, shrink_split), axis=1
    )
    packed = padded(packed, (row_pad, col_pad))
    packed = jnp.concatenate((packed, padded(vectors[None], (16, col_pad))), axis=0)
    whole, both = gather_start(packed, jnp.concatenate((tokens, cotangent), axis=1))
    tokens_all = both[:, :, :D].reshape(group, D)
    upstream_all = both[:, :, D:].reshape(group, D)

    mine = whole[:, :dr]
    expand_rows = mine[:, :, : 4 * dc].transpose(1, 0, 2).reshape(dr, FF)
    attend_rows = (
        mine[:, :, 4 * dc : 7 * dc].reshape(N, dr, 3, dc).transpose(1, 2, 0, 3).reshape(dr, 3, D)
    )
    output_rows = mine[:, :, 7 * dc : 8 * dc].transpose(1, 0, 2).reshape(dr, D)
    shrink_rows = (
        mine[:, :, 8 * dc : 12 * dc].reshape(N, dr, 4, dc).transpose(2, 1, 0, 3).reshape(4 * dr, D)
    )

    attend_out = (
        padded(attend_rows, (dr, 3, S * hw)).reshape(dr, 3, S, hw).transpose(2, 0, 1, 3)
    ).reshape(S, dr, 3 * hw)
    attend_cols = swap_seq(attend_out).reshape(D, 3 * hw)
    expand_out = expand_rows.reshape(dr, S, hq).transpose(1, 0, 2)
    expand_cols = swap_seq(expand_out).reshape(D, hq)
    output_and = jnp.concatenate(
        (padded(output_rows, (row_pad, D)), padded(whole[:, row_pad, :vn], (up(N, 16), D))), axis=0
    )
    output_and_all = gather_seq(output_and)
    output_all = output_and_all[:, :dr].reshape(D, D)
    output_heads = lax.dynamic_slice_in_dim(
        padded(output_all, (S * hw, D)), place * hw, hw, 0
    )
    flat = output_and_all[:, row_pad : row_pad + N, :vn].transpose(1, 0, 2).reshape(-1)
    table = flat[: 8 * D].astype(F32).reshape(8, D)
    fc_bias = flat[8 * D :].astype(F32)

    def head_part(vector):
        return lax.dynamic_slice_in_dim(padded(vector, (S * hw,)), place * hw, hw, 0)

    normed_all, _ = layer_norm(tokens_all.astype(F32))
    hidden_one_all = (normed_all * table[0] + table[1]).astype(BF)
    inputs32 = tokens.astype(F32)
    normed_one, inverse_one = layer_norm(inputs32)
    projected = dot(hidden_one_all, attend_cols, 1, 0)
    bias = jnp.concatenate((head_part(table[2]), jnp.zeros((hw,), F32), head_part(table[3])))
    triple = (projected + bias).astype(BF).reshape(group, 3, heads, HD).transpose(1, 2, 0, 3)
    query, key, value = triple[0], triple[1], triple[2]
    segment = segment_ids.reshape(-1)
    pos = jnp.arange(group, dtype=jnp.int32)
    allowed = (pos[None, :] <= pos[:, None]) & (segment[None, :] == segment[:, None])
    scores = jnp.einsum("htd,hgd->htg", query, key, preferred_element_type=F32) * 0.125
    scores = jnp.where(allowed[None], scores, -jnp.inf)
    peak = jnp.max(scores, axis=-1, keepdims=True)
    unscaled = jnp.exp(scores - peak)
    probs = unscaled / jnp.sum(unscaled, axis=-1, keepdims=True)
    probs_low = probs.astype(BF)
    context = jnp.einsum("htg,hgd->htd", probs_low, value, preferred_element_type=F32).astype(BF)
    context_cols = context.transpose(1, 0, 2).reshape(group, hw)
    attn = dot(context_cols, output_heads, 1, 0).astype(BF)
    residual = inputs32 + sum_seq(attn.reshape(S, rows, D)) + table[4]
    normed_two, inverse_two = layer_norm(residual)
    hidden_two = (normed_two * table[5] + table[6]).astype(BF)
    hidden_two_all = gather_seq(hidden_two).reshape(group, D)
    hidden_bias = lax.dynamic_slice_in_dim(fc_bias, place * hq, hq, 0)
    pre = dot(hidden_two_all, expand_cols, 1, 0) + hidden_bias
    activated, slope = gelu_parts(pre)
    activated_low = activated.astype(BF)
    branch = dot(activated_low, shrink_rows, 1, 0).astype(BF)
    upstream = cotangent.astype(F32)
    pre_grad = dot(upstream_all, shrink_rows, 1, 1) * slope
    pre_low = pre_grad.astype(BF)
    hidden_two_grad = sum_seq(dot(pre_low, expand_cols, 1, 1).astype(BF).reshape(S, rows, D))
    mixed = (residual + sum_seq(branch.reshape(S, rows, D)) + table[7]).astype(BF)
    shrink_grad = dot(activated_low, upstream_all, 0, 0).astype(BF)
    expand_grad = dot(hidden_two_all, pre_low, 0, 0).astype(BF)
    expand_grad = swap_seq(expand_grad.reshape(S, dr, hq))
    residual_grad = upstream + norm_back(hidden_two_grad, normed_two, inverse_two, table[5])
    residual_all = gather_seq(residual_grad.astype(BF)).reshape(group, D)
    grad = dot(residual_all, output_heads, 1, 1).astype(BF)
    grad = grad.reshape(group, heads, HD).transpose(1, 0, 2)
    row_dots = jnp.sum(grad.astype(F32) * context.astype(F32), axis=-1, keepdims=True)
    prob_grad = jnp.einsum("htd,hgd->htg", grad, value, preferred_element_type=F32)
    score_grad = (probs * (prob_grad - row_dots)).astype(BF)
    query_grad = jnp.einsum("htg,hgd->thd", score_grad, key, preferred_element_type=F32) * 0.125
    key_grad = jnp.einsum("htg,htd->ghd", score_grad, query, preferred_element_type=F32) * 0.125
    value_grad = jnp.einsum("htg,htd->ghd", probs_low, grad, preferred_element_type=F32)
    query_grad, key_grad, value_grad = (
        g.reshape(group, hw) for g in (query_grad, key_grad, value_grad)
    )
    joined = jnp.concatenate((query_grad, key_grad, value_grad), axis=1).astype(BF)
    hidden_one_grad = sum_seq(dot(joined, attend_cols, 1, 1).astype(BF).reshape(S, rows, D))
    attend_grad = dot(hidden_one_all, joined, 0, 0).astype(BF)
    attend_grad = swap_seq(attend_grad.reshape(S, dr, 3 * hw))
    output_grad = dot(context_cols, residual_all, 0, 0).astype(BF)
    output_grad = lax.dynamic_slice_in_dim(
        gather_seq(output_grad).reshape(S * hw, D), place * dr, dr, 0
    )
    tokens_grad = residual_grad + norm_back(hidden_one_grad, normed_one, inverse_one, table[0])

    attend_grad = attend_grad.reshape(S, dr, 3, hw).transpose(1, 2, 0, 3).reshape(dr, 3, S * hw)
    attend_grad = attend_grad[:, :, :D].reshape(dr, 3, N, dc).transpose(2, 0, 1, 3)
    expand_grad = expand_grad.reshape(S, dr, N // S, fc).transpose(0, 2, 1, 3).reshape(N, dr, fc)
    output_grad = output_grad.reshape(dr, N, dc).transpose(1, 0, 2)
    shrink_grad = shrink_grad.reshape(4, dr, N, dc).transpose(2, 1, 0, 3).reshape(N, dr, 4 * dc)
    packed_grad = jnp.concatenate(
        (expand_grad, attend_grad.reshape(N, dr, 3 * dc), output_grad, shrink_grad), axis=2
    )

    def spread(vector, total, start):
        return lax.dynamic_update_slice(jnp.zeros((total,), F32), vector, (start,))

    vector_grad = jnp.concatenate(
        (
            jnp.sum(hidden_one_grad * normed_one, axis=0),
            jnp.sum(hidden_one_grad, axis=0),
            spread(jnp.sum(query_grad, axis=0), S * hw, place * hw)[:D],
            spread(jnp.sum(value_grad, axis=0), S * hw, place * hw)[:D],
            jnp.sum(residual_grad, axis=0),
            jnp.sum(hidden_two_grad * normed_two, axis=0),
            jnp.sum(hidden_two_grad, axis=0),
            jnp.sum(upstream, axis=0),
            spread(jnp.sum(pre_grad, axis=0), FF, place * hq),
        )
    )
    by_owner = vector_grad.reshape(N, S, vn).transpose(1, 0, 2)
    by_owner = padded(by_owner, (S, up(N, 16), up(vn, 128)))
    vector_part = sum_seq(by_owner)[:N].astype(BF)
    vector_part = padded(vector_part[:, None, :], (N, 16, col_pad))
    packed_grad = jnp.concatenate(
        (padded(packed_grad, (N, row_pad, col_pad)), vector_part), axis=1
    )
    total = sum_dp(packed_grad)
    weight_sum = total[:dr]
    return (
        mixed,
        tokens_grad,
        weight_sum[:, 4 * dc : 7 * dc].reshape(dr, 3, dc),
        weight_sum[:, 7 * dc : 8 * dc],
        weight_sum[:, : 4 * dc],
        weight_sum[:, 8 * dc : 12 * dc].reshape(dr, 4, dc).transpose(1, 0, 2).reshape(4 * dr, dc),
        total[row_pad, :vn],
    )


def solution(mesh):
    global IDS
    IDS = itertools.count()
    return jax.shard_map(
        body,
        mesh=mesh,
        in_specs=(
            P(("dp", "seq"), None),
            P("dp", None),
            P("seq", None, "dp"),
            P("seq", "dp"),
            P("seq", "dp"),
            P("seq", "dp"),
            P(("dp", "seq")),
            P(("dp", "seq"), None),
        ),
        out_specs=(
            P(("dp", "seq"), None),
            P(("dp", "seq"), None),
            P("seq", None, "dp"),
            P("seq", "dp"),
            P("seq", "dp"),
            P("seq", "dp"),
            P(("dp", "seq")),
        ),
        check_vma=False,
    )
```

```python
import itertools
import math
import jax
import jax.numpy as jnp
from jax import lax
from jax.experimental import pallas as pl
from jax.experimental.pallas import tpu as pltpu
from jax.sharding import PartitionSpec as P

D = 1088
H = 17
HD = 64
FF = 4352
EPS = 1e-05
BF = jnp.bfloat16
F32 = jnp.float32


def layer_norm(values):
    centre = values - jnp.mean(values, axis=-1, keepdims=True)
    inverse = lax.rsqrt(jnp.mean(centre * centre, axis=-1, keepdims=True) + EPS)
    return (centre * inverse, inverse)


def norm_back(upstream, normed, inverse, gain):
    scaled = upstream * gain
    return (
        scaled
        - jnp.mean(scaled, axis=-1, keepdims=True)
        - normed * jnp.mean(scaled * normed, axis=-1, keepdims=True)
    ) * inverse


def gelu_parts(pre):
    normal_cdf = 0.5 * (1.0 + lax.erf(pre * 0.7071067811865476))
    density = jnp.exp(-0.5 * pre * pre) * 0.3989422804014327
    return (pre * normal_cdf, normal_cdf + pre * density)


MESH = pl.DeviceIdType.MESH
IDS = itertools.count()
LIMIT = 48 * 2**20


def greet(targets):
    barrier = pltpu.get_barrier_semaphore()
    for target in targets:
        pl.semaphore_signal(barrier, inc=1, device_id=target, device_id_type=MESH)
    pl.semaphore_wait(barrier, len(targets))


def send(src, dst, send_sem, recv_sem, target):
    copy = pltpu.make_async_remote_copy(
        src_ref=src,
        dst_ref=dst,
        send_sem=send_sem,
        recv_sem=recv_sem,
        device_id=target,
        device_id_type=MESH,
    )
    copy.start()
    return copy


def run_kernel(kernel, out_shapes, scratch, *args):
    cost = sum(16 * a.size * a.dtype.itemsize for a in args) + 2**24
    return pl.pallas_call(
        kernel,
        out_shape=out_shapes,
        in_specs=[pl.BlockSpec(memory_space=pltpu.VMEM)] * len(args),
        out_specs=jax.tree.map(lambda _: pl.BlockSpec(memory_space=pltpu.VMEM), out_shapes),
        scratch_shapes=scratch,
        cost_estimate=pl.CostEstimate(flops=0, bytes_accessed=cost, transcendentals=0),
        compiler_params=pltpu.CompilerParams(
            collective_id=next(IDS), has_side_effects=True, vmem_limit_bytes=LIMIT
        ),
    )(*args)


def dma(*shape):
    return pltpu.SemaphoreType.DMA(shape)


def gather_seq_steps(n, src, dst, local, sends, recvs):
    chips = n // 2
    me = lax.axis_index("seq")
    x, core = me // 2, me % 2
    other = {"seq": x * 2 + (1 - core)}
    own = pltpu.make_async_copy(src, dst.at[me], local)
    own.start()
    across = []
    for k in range(1, chips):
        target = {"seq": lax.rem(x + k, chips) * 2 + core}
        across.append(send(src, dst.at[me], sends.at[0, k], recvs.at[0, k], target))
    inner = [send(src, dst.at[me], sends.at[1, 0], recvs.at[1, 0], other)]

    def finish():
        for k in range(1, chips):
            across[k - 1].wait_recv()
            slot = lax.rem(x + chips - k, chips) * 2 + core
            inner.append(
                send(dst.at[slot], dst.at[slot], sends.at[1, k], recvs.at[1, k], other)
            )
        for copy in inner:
            copy.wait_recv()
        for copy in across + inner:
            copy.wait_send()
        own.wait()

    return finish


def seq_partners(n):
    me = lax.axis_index("seq")
    x, core = me // 2, me % 2
    chips = n // 2
    return [{"seq": x * 2 + (1 - core)}] + [
        {"seq": lax.rem(x + k, chips) * 2 + core} for k in range(1, chips)
    ]


def gather_seq(values):
    n = lax.axis_size("seq")

    def kernel(src, dst, local, sends, recvs):
        greet(seq_partners(n))
        gather_seq_steps(n, src, dst, local, sends, recvs)()

    return run_kernel(
        kernel,
        jax.ShapeDtypeStruct((n,) + values.shape, values.dtype),
        [pltpu.SemaphoreType.DMA, dma(2, n // 2), dma(2, n // 2)],
        values,
    )


def swap_seq(values):
    n = lax.axis_size("seq")

    def kernel(src, dst, local, sends, recvs):
        me = lax.axis_index("seq")
        greet([{"seq": lax.rem(me + k, n)} for k in range(1, n)])
        own = pltpu.make_async_copy(src.at[me], dst.at[me], local)
        own.start()
        copies = []
        for k in range(n - 1, 0, -1):
            to = lax.rem(me + k, n)
            copies.append(
                send(src.at[to], dst.at[me], sends.at[k - 1], recvs.at[k - 1], {"seq": to})
            )
        for copy in copies:
            copy.wait_recv()
        for copy in copies:
            copy.wait_send()
        own.wait()

    return run_kernel(
        kernel,
        jax.ShapeDtypeStruct(values.shape, values.dtype),
        [pltpu.SemaphoreType.DMA, dma(n - 1), dma(n - 1)],
        values,
    )


def sum_seq(values):
    return jnp.sum(swap_seq(values).astype(F32), axis=0)


def dp_layout():
    n = lax.axis_size("dp")
    wide = math.isqrt(n // 2)
    return n // wide, wide


def pieces(size, parts):
    units = size // 16
    edges = [units * i // parts * 16 for i in range(parts + 1)]
    return [(a, b - a) for a, b in zip(edges, edges[1:])]


def dp_partners(deep, wide):
    me = lax.axis_index("dp")
    z, y = me // wide, me % wide
    return [{"dp": lax.rem(z + k, deep) * wide + y} for k in range(1, deep)] + [
        {"dp": z * wide + lax.rem(y + k, wide)} for k in range(1, wide)
    ]


def gather_start(values, both):
    n = lax.axis_size("seq")
    deep, wide = dp_layout()
    chunks = pieces(values.shape[0], 3)

    def kernel(src, act, dst, act_dst, local, s_sends, s_recvs, z_send, z_recv, y_send, y_recv):
        me = lax.axis_index("dp")
        z, y = me // wide, me % wide
        greet(dp_partners(deep, wide) + seq_partners(n))
        finish = gather_seq_steps(n, act, act_dst, local.at[0], s_sends, s_recvs)
        own = pltpu.make_async_copy(src, dst.at[me], local.at[1])
        own.start()
        first, second = {}, []
        for c, (start, size) in enumerate(chunks):
            part = pl.ds(start, size)
            for k in range(1, deep):
                to = {"dp": lax.rem(z + k, deep) * wide + y}
                first[c, k] = send(
                    src.at[part], dst.at[me, part], z_send.at[c, k], z_recv.at[c, k], to
                )
            for j in range(1, wide):
                to = {"dp": z * wide + lax.rem(y + j, wide)}
                second.append(
                    send(
                        src.at[part], dst.at[me, part], y_send.at[c, j, 0], y_recv.at[c, j, 0], to
                    )
                )
        for c, (start, size) in enumerate(chunks):
            part = pl.ds(start, size)
            for k in range(1, deep):
                first[c, k].wait_recv()
                slot = lax.rem(z + deep - k, deep) * wide + y
                for j in range(1, wide):
                    to = {"dp": z * wide + lax.rem(y + j, wide)}
                    block = dst.at[slot, part]
                    second.append(
                        send(block, block, y_send.at[c, j, k], y_recv.at[c, j, k], to)
                    )
        finish()
        for copy in second:
            copy.wait_recv()
        for copy in list(first.values()) + second:
            copy.wait_send()
        own.wait()

    m = len(chunks)
    return run_kernel(
        kernel,
        (
            jax.ShapeDtypeStruct((deep * wide,) + values.shape, values.dtype),
            jax.ShapeDtypeStruct((n,) + both.shape, both.dtype),
        ),
        [dma(2), dma(2, n // 2), dma(2, n // 2)]
        + [dma(m, deep), dma(m, deep), dma(m, wide, deep), dma(m, wide, deep)],
        values,
        both,
    )


def sum_dp(values):
    deep, wide = dp_layout()
    rows, cols = values.shape[1:]
    chunks = pieces(rows, 3)

    def kernel(src, out, y_buf, z_out, z_buf, y_send, y_recv, z_send, z_recv):
        me = lax.axis_index("dp")
        z, y = me // wide, me % wide
        greet(dp_partners(deep, wide))
        order = list(range(1, deep)) + [0]
        first, second = {}, []
        for c, (start, size) in enumerate(chunks):
            part = pl.ds(start, size)
            for k in order:
                for j in range(1, wide):
                    there = lax.rem(y + j, wide)
                    first[c, k, j] = send(
                        src.at[lax.rem(z + k, deep) * wide + there, part],
                        y_buf.at[j - 1, k, part],
                        y_send.at[c, j, k],
                        y_recv.at[c, j, k],
                        {"dp": z * wide + there},
                    )
        for c, (start, size) in enumerate(chunks):
            part = pl.ds(start, size)
            for k in order:
                for j in range(1, wide):
                    first[c, k, j].wait_recv()
                block = lax.rem(z + k, deep) * wide + y

                @pl.loop(0, size // 16)
                def _(i):
                    strip = pl.ds(pl.multiple_of(start + i * 16, 16), 16)
                    total = src[block, strip, :].astype(F32)
                    for j in range(1, wide):
                        total = total + y_buf[j - 1, k, strip, :].astype(F32)
                    if k == 0:
                        out[strip, :] = total
                    else:
                        z_out[k - 1, strip, :] = total.astype(z_out.dtype)

                if k > 0:
                    second.append(
                        send(
                            z_out.at[k - 1, part],
                            z_buf.at[k - 1, part],
                            z_send.at[c, k],
                            z_recv.at[c, k],
                            {"dp": block},
                        )
                    )
        for c, (start, size) in enumerate(chunks):
            for k in range(1, deep):
                second[c * (deep - 1) + k - 1].wait_recv()

            @pl.loop(0, size // 16)
            def _(i):
                strip = pl.ds(pl.multiple_of(start + i * 16, 16), 16)
                total = out[strip, :]
                for k in range(1, deep):
                    total = total + z_buf[k - 1, strip, :].astype(F32)
                out[strip, :] = total

        for copy in list(first.values()) + second:
            copy.wait_send()

    m = len(chunks)
    return run_kernel(
        kernel,
        jax.ShapeDtypeStruct((rows, cols), F32),
        [
            pltpu.VMEM((wide - 1, deep, rows, cols), BF),
            pltpu.VMEM((deep - 1, rows, cols), BF),
            pltpu.VMEM((deep - 1, rows, cols), BF),
            dma(m, wide, deep),
            dma(m, wide, deep),
            dma(m, deep),
            dma(m, deep),
        ],
        values,
    )


def dot(a, b, ca, cb):
    return lax.dot_general(a, b, (((ca,), (cb,)), ((), ())), preferred_element_type=F32)


def up(value, step):
    return -(-value // step) * step


def padded(values, shape):
    return jnp.pad(values, [(0, n - m) for m, n in zip(values.shape, shape)])


def body(
    tokens,
    segment_ids,
    attend_weight,
    output_weight,
    expand_weight,
    shrink_weight,
    vectors,
    cotangent,
):
    rows = tokens.shape[0]
    S = lax.axis_size("seq")
    N = lax.axis_size("dp")
    group = rows * S
    place = lax.axis_index("seq")
    dr = D // S
    dc = D // N
    fc = FF // N
    hq = FF // S
    heads = -(-H // S)
    hw = heads * HD
    vn = vectors.shape[0]
    row_pad = up(dr, 16)
    cols = 4 * dc
    col_pad = up(max(cols, vn), 128)
    wide = N // S

    moves = [
        (p * S + s, ((p % wide) * S + s) * S + p // wide) for p in range(N) for s in range(S)
    ]
    expand_block = lax.ppermute(expand_weight, ("dp", "seq"), moves)
    expand_parts = lax.all_gather(expand_block, "dp", axis=0, tiled=False)
    expand_parts = expand_parts.reshape(wide, D, fc)
    shrink_t = lax.all_gather(shrink_weight.T, "dp", axis=0, tiled=False).reshape(D, hq)

    packed = jnp.concatenate((attend_weight.reshape(dr, 3 * dc), output_weight), axis=1)
    packed = padded(packed, (row_pad, col_pad))
    packed = jnp.concatenate((packed, padded(vectors[None], (16, col_pad))), axis=0)
    whole, both = gather_start(packed, jnp.concatenate((tokens, cotangent), axis=1))
    tokens_all = both[:, :, :D].reshape(group, D)
    upstream_all = both[:, :, D:].reshape(group, D)

    mine = whole[:, :dr]
    attend_rows = (
        mine[:, :, : 3 * dc].reshape(N, dr, 3, dc).transpose(1, 2, 0, 3).reshape(dr, 3, D)
    )
    output_rows = mine[:, :, 3 * dc : 4 * dc].transpose(1, 0, 2).reshape(dr, D)

    attend_out = (
        padded(attend_rows, (dr, 3, S * hw)).reshape(dr, 3, S, hw).transpose(2, 0, 1, 3)
    ).reshape(S, dr, 3 * hw)
    attend_cols = swap_seq(attend_out).reshape(D, 3 * hw)
    output_and = jnp.concatenate(
        (padded(output_rows, (row_pad, D)), padded(whole[:, row_pad, :vn], (up(N, 16), D))), axis=0
    )
    output_and_all = gather_seq(output_and)
    output_all = output_and_all[:, :dr].reshape(D, D)
    output_heads = lax.dynamic_slice_in_dim(
        padded(output_all, (S * hw, D)), place * hw, hw, 0
    )
    flat = output_and_all[:, row_pad : row_pad + N, :vn].transpose(1, 0, 2).reshape(-1)
    table = flat[: 8 * D].astype(F32).reshape(8, D)
    fc_bias = flat[8 * D :].astype(F32)

    def head_part(vector):
        return lax.dynamic_slice_in_dim(padded(vector, (S * hw,)), place * hw, hw, 0)

    normed_all, _ = layer_norm(tokens_all.astype(F32))
    hidden_one_all = (normed_all * table[0] + table[1]).astype(BF)
    inputs32 = tokens.astype(F32)
    normed_one, inverse_one = layer_norm(inputs32)
    projected = dot(hidden_one_all, attend_cols, 1, 0)
    bias = jnp.concatenate((head_part(table[2]), jnp.zeros((hw,), F32), head_part(table[3])))
    triple = (projected + bias).astype(BF).reshape(group, 3, heads, HD).transpose(1, 2, 0, 3)
    query, key, value = triple[0], triple[1], triple[2]
    segment = segment_ids.reshape(-1)
    pos = jnp.arange(group, dtype=jnp.int32)
    allowed = (pos[None, :] <= pos[:, None]) & (segment[None, :] == segment[:, None])
    scores = jnp.einsum("htd,hgd->htg", query, key, preferred_element_type=F32) * 0.125
    scores = jnp.where(allowed[None], scores, -jnp.inf)
    peak = jnp.max(scores, axis=-1, keepdims=True)
    unscaled = jnp.exp(scores - peak)
    probs = unscaled / jnp.sum(unscaled, axis=-1, keepdims=True)
    probs_low = probs.astype(BF)
    context = jnp.einsum("htg,hgd->htd", probs_low, value, preferred_element_type=F32).astype(BF)
    context_cols = context.transpose(1, 0, 2).reshape(group, hw)
    attn = dot(context_cols, output_heads, 1, 0).astype(BF)
    residual = inputs32 + sum_seq(attn.reshape(S, rows, D)) + table[4]
    normed_two, inverse_two = layer_norm(residual)
    hidden_two = (normed_two * table[5] + table[6]).astype(BF)
    hidden_two_all = gather_seq(hidden_two).reshape(group, D)
    hidden_bias = lax.dynamic_slice_in_dim(fc_bias, place * hq, hq, 0)
    pre = jnp.concatenate([dot(hidden_two_all, e, 1, 0) for e in expand_parts], axis=1)
    pre = pre + hidden_bias
    activated, slope = gelu_parts(pre)
    activated_low = activated.astype(BF)
    branch = dot(activated_low, shrink_t, 1, 1).astype(BF)
    upstream = cotangent.astype(F32)
    pre_grad = dot(upstream_all, shrink_t, 1, 0) * slope
    pre_low = pre_grad.astype(BF)
    pre_parts = [pre_low[:, j * fc : (j + 1) * fc] for j in range(wide)]
    hidden_grad = sum(dot(g, e, 1, 1) for g, e in zip(pre_parts, expand_parts))
    hidden_two_grad = sum_seq(hidden_grad.astype(BF).reshape(S, rows, D))
    branch = lax.psum_scatter(branch.reshape(S, rows, D), "seq", scatter_dimension=0, tiled=False)
    mixed = (residual + branch.astype(F32) + table[7]).astype(BF)
    shrink_grad = dot(upstream_all, activated_low, 0, 0).astype(BF).reshape(N, dc, hq)
    shrink_sum = lax.psum_scatter(shrink_grad, "dp", scatter_dimension=0, tiled=False)
    expand_grad = jnp.stack([dot(hidden_two_all, g, 0, 0).astype(BF) for g in pre_parts])
    expand_sum = lax.psum_scatter(
        expand_grad.reshape(N, dr, fc), "dp", scatter_dimension=0, tiled=False
    )
    expand_sum = lax.ppermute(expand_sum, ("dp", "seq"), [(b, a) for a, b in moves])
    residual_grad = upstream + norm_back(hidden_two_grad, normed_two, inverse_two, table[5])
    residual_all = gather_seq(residual_grad.astype(BF)).reshape(group, D)
    grad = dot(residual_all, output_heads, 1, 1).astype(BF)
    grad = grad.reshape(group, heads, HD).transpose(1, 0, 2)
    row_dots = jnp.sum(grad.astype(F32) * context.astype(F32), axis=-1, keepdims=True)
    prob_grad = jnp.einsum("htd,hgd->htg", grad, value, preferred_element_type=F32)
    score_grad = (probs * (prob_grad - row_dots)).astype(BF)
    query_grad = jnp.einsum("htg,hgd->thd", score_grad, key, preferred_element_type=F32) * 0.125
    key_grad = jnp.einsum("htg,htd->ghd", score_grad, query, preferred_element_type=F32) * 0.125
    value_grad = jnp.einsum("htg,htd->ghd", probs_low, grad, preferred_element_type=F32)
    query_grad, key_grad, value_grad = (
        g.reshape(group, hw) for g in (query_grad, key_grad, value_grad)
    )
    joined = jnp.concatenate((query_grad, key_grad, value_grad), axis=1).astype(BF)
    hidden_one_grad = sum_seq(dot(joined, attend_cols, 1, 1).astype(BF).reshape(S, rows, D))
    attend_grad = dot(hidden_one_all, joined, 0, 0).astype(BF)
    attend_grad = swap_seq(attend_grad.reshape(S, dr, 3 * hw))
    output_grad = dot(context_cols, residual_all, 0, 0).astype(BF)
    output_grad = lax.dynamic_slice_in_dim(
        gather_seq(output_grad).reshape(S * hw, D), place * dr, dr, 0
    )
    tokens_grad = residual_grad + norm_back(hidden_one_grad, normed_one, inverse_one, table[0])

    attend_grad = attend_grad.reshape(S, dr, 3, hw).transpose(1, 2, 0, 3).reshape(dr, 3, S * hw)
    attend_grad = attend_grad[:, :, :D].reshape(dr, 3, N, dc).transpose(2, 0, 1, 3)
    output_grad = output_grad.reshape(dr, N, dc).transpose(1, 0, 2)
    packed_grad = jnp.concatenate((attend_grad.reshape(N, dr, 3 * dc), output_grad), axis=2)

    def spread(vector, total, start):
        return lax.dynamic_update_slice(jnp.zeros((total,), F32), vector, (start,))

    vector_grad = jnp.concatenate(
        (
            jnp.sum(hidden_one_grad * normed_one, axis=0),
            jnp.sum(hidden_one_grad, axis=0),
            spread(jnp.sum(query_grad, axis=0), S * hw, place * hw)[:D],
            spread(jnp.sum(value_grad, axis=0), S * hw, place * hw)[:D],
            jnp.sum(residual_grad, axis=0),
            jnp.sum(hidden_two_grad * normed_two, axis=0),
            jnp.sum(hidden_two_grad, axis=0),
            jnp.sum(upstream, axis=0),
            spread(jnp.sum(pre_grad, axis=0), FF, place * hq),
        )
    )
    by_owner = vector_grad.reshape(N, S, vn).transpose(1, 0, 2)
    by_owner = padded(by_owner, (S, up(N, 16), up(vn, 128)))
    vector_part = sum_seq(by_owner)[:N].astype(BF)
    vector_part = padded(vector_part[:, None, :], (N, 16, col_pad))
    packed_grad = jnp.concatenate(
        (padded(packed_grad, (N, row_pad, col_pad)), vector_part), axis=1
    )
    total = sum_dp(packed_grad)
    weight_sum = total[:dr]
    return (
        mixed,
        tokens_grad,
        weight_sum[:, : 3 * dc].reshape(dr, 3, dc),
        weight_sum[:, 3 * dc : 4 * dc],
        expand_sum.astype(F32),
        shrink_sum.astype(F32).T,
        total[row_pad, :vn],
    )


def solution(mesh):
    global IDS
    IDS = itertools.count()
    return jax.shard_map(
        body,
        mesh=mesh,
        in_specs=(
            P(("dp", "seq"), None),
            P("dp", None),
            P("seq", None, "dp"),
            P("seq", "dp"),
            P("seq", "dp"),
            P("seq", "dp"),
            P(("dp", "seq")),
            P(("dp", "seq"), None),
        ),
        out_specs=(
            P(("dp", "seq"), None),
            P(("dp", "seq"), None),
            P("seq", None, "dp"),
            P("seq", "dp"),
            P("seq", "dp"),
            P("seq", "dp"),
            P(("dp", "seq")),
        ),
        check_vma=False,
    )
```
